32 devices in a mesh: dp: 8 (over y, x, core), blk: 4 (over z).
Axes of the slice: x: 2, y: 2, z: 4, core: 2. Of those that a mesh axis runs over, the one named last changes fastest.
Arguments:
- prod_feat: bfloat16 [8, 3072, 768], P('dp', 'blk'), may hold values from -23 to 23
- prec_feat: bfloat16 [8, 3072, 768], P('dp', 'blk'), may hold values from -23 to 23
- matched: int32 [8, 3072], P('dp', 'blk'), may hold values from 0 to 3071, each once within a row
- row_weight: float32 [8, 3072], P('dp', 'blk'), may hold values from 0.2 to 28, as said below
- proj_prod: bfloat16 [768, 1024], replicated, may hold values from -0.21875 to 0.21875
- proj_prec: bfloat16 [768, 1024], replicated, may hold values from -0.21875 to 0.21875
Outputs:
- loss_value: float32 [], replicated
- grad_prod: float32 [768, 1024], P('dp', 'blk')
- grad_prec: float32 [768, 1024], P('dp', 'blk')
The draws below stay inside these ranges and needn't reach their ends.
Inputs may be any that keep to these rules, and one draw needn't show every extreme that they name: `matched`: in each of the 8 groups the 3072 values are a permutation of 0 to 3071. `row_weight`: positive.
All inputs are finite; a program needn't handle non-finite values.
Results may differ from the reference program's by a relative error of at most 0.0027.
Values may be sent and summed in bfloat16 or wider, within the bound.
A program may use at most 128 MiB of HBM per device.

```python
import jax
import jax.numpy as jnp
from jax import lax

FEAT = 768
EMBED = 1024
GROUP = 3072
N_DP = 8


def feature_draw(key):
    col_key, val_key = jax.random.split(key, 2)
    exponent = jax.random.uniform(col_key, (FEAT,), jnp.float32, 0.0, 1.5)
    scales = 10.0 ** (exponent - 0.75)
    values = jax.random.truncated_normal(val_key, -4.0, 4.0, (N_DP, GROUP, FEAT), jnp.float32)
    return (values * scales).astype(jnp.bfloat16)


def draw_prod_feat(key, part):
    return feature_draw(jax.random.fold_in(key, 11))


def draw_prec_feat(key, part):
    return feature_draw(jax.random.fold_in(key, 23))


def draw_row_weight(key, part):
    base_key = jax.random.fold_in(key, 37)
    base = jnp.exp(jax.random.uniform(base_key, (N_DP, GROUP), jnp.float32, -1.2, 1.1))
    group_frac = jnp.arange(N_DP, dtype=jnp.float32) / max(N_DP - 1, 1)
    row_frac = jnp.arange(GROUP, dtype=jnp.float32) / max(GROUP - 1, 1)
    ramp = (3.0 ** group_frac)[:, None] * (3.0 ** row_frac)[None, :]
    return base * ramp


def bell_draw(stream_key, dims, deviation, limit, held_as=jnp.bfloat16):
    return jnp.clip(deviation * jax.random.normal(stream_key, dims, jnp.float32), -limit, limit).astype(held_as)


def setup_inputs(seed: int = 0) -> dict:
    splits = jax.random.split(jax.random.key(seed), 7)
    prod_feat = draw_prod_feat(jax.random.fold_in(splits[6], 71), 0)
    prec_feat = draw_prec_feat(jax.random.fold_in(splits[6], 71), 0)
    matched = jax.vmap(lambda own: jax.random.permutation(own, GROUP))(jax.random.split(splits[2], N_DP)).reshape((N_DP, GROUP)).astype(jnp.int32)
    row_weight = draw_row_weight(jax.random.fold_in(splits[6], 71), 0)
    proj_prod = bell_draw(splits[4], (FEAT, EMBED), FEAT ** -0.5, 0.21875)
    proj_prec = bell_draw(splits[5], (FEAT, EMBED), FEAT ** -0.5, 0.21875)
    return dict(prod_feat=prod_feat, prec_feat=prec_feat, matched=matched, row_weight=row_weight, proj_prod=proj_prod, proj_prec=proj_prec)


EPS = 1e-06
LOGIT_SCALE = 50.0

def embed_rows(features, weight):
    projected_raw = jnp.dot(features, weight, preferred_element_type=jnp.float32)
    radius = jnp.sqrt(lax.optimization_barrier(jnp.sum(projected_raw * projected_raw, axis=1, keepdims=True)) + EPS)
    unit_vec = projected_raw / radius
    return (unit_vec, unit_vec.astype(jnp.bfloat16), radius)

def similarity(queries, key_rows):
    return LOGIT_SCALE * lax.dot_general(queries, key_rows, (((1,), (1,)), ((), ())), preferred_element_type=jnp.float32)

def coefficient(scores, matches, weights, totals):
    probability = jnp.exp(scores - LOGIT_SCALE) / totals[:, None]
    return (weights[:, None] * (probability - matches.astype(jnp.float32))).astype(jnp.bfloat16)

def back_norm(unit_vec, radius, gradient):
    projected = lax.optimization_barrier(jnp.sum(unit_vec * gradient, axis=1, keepdims=True))
    return ((gradient - unit_vec * projected) / radius).astype(jnp.bfloat16)

def reference(prod_feat, prec_feat, matched, row_weight, proj_prod, proj_prec):

    def one_group(inputs):
        feat_prod, feat_prec, targets, weights = inputs
        unit_prod, unit16_prod, radius_prod = embed_rows(feat_prod, proj_prod)
        unit_prec, unit16_prec, radius_prec = embed_rows(feat_prec, proj_prec)
        scores = similarity(unit16_prod, unit16_prec)
        columns = jnp.arange(GROUP, dtype=jnp.int32)
        matches = targets[:, None] == columns[None, :]
        totals = lax.optimization_barrier(jnp.sum(jnp.exp(scores - LOGIT_SCALE), axis=1))
        positive = lax.optimization_barrier(jnp.sum(jnp.where(matches, scores, 0.0), axis=1))
        losses = LOGIT_SCALE + jnp.log(totals) - positive
        coeffs = coefficient(scores, matches, weights, totals)
        grad_unit_prod = LOGIT_SCALE * jnp.dot(coeffs, unit16_prec, preferred_element_type=jnp.float32)
        grad_unit_prec = LOGIT_SCALE * lax.dot_general(coeffs, unit16_prod, (((0,), (0,)), ((), ())), preferred_element_type=jnp.float32)
        dir_prod = back_norm(unit_prod, radius_prod, grad_unit_prod)
        dir_prec = back_norm(unit_prec, radius_prec, grad_unit_prec)
        head_prod = lax.dot_general(feat_prod, dir_prod, (((0,), (0,)), ((), ())), preferred_element_type=jnp.float32)
        head_prec = lax.dot_general(feat_prec, dir_prec, (((0,), (0,)), ((), ())), preferred_element_type=jnp.float32)
        return (jnp.sum(weights * losses), jnp.sum(weights), head_prod, head_prec)
    loss_sums, weight_sums, heads_prod, heads_prec = lax.map(one_group, (prod_feat, prec_feat, matched, row_weight))
    weight_total = jnp.sum(weight_sums)
    return (jnp.sum(loss_sums) / weight_total, lax.optimization_barrier(jnp.sum(heads_prod, axis=0)) / weight_total, lax.optimization_barrier(jnp.sum(heads_prec, axis=0)) / weight_total)
```

```python
import functools
import math

import jax
import jax.numpy as jnp
from jax import lax
from jax.experimental import pallas as pl
from jax.experimental.pallas import tpu as pltpu
from jax.sharding import PartitionSpec as P

EPS = 1e-06
LOGIT_SCALE = 50.0
MESH = pl.DeviceIdType.MESH
F32 = jnp.float32
BF16 = jnp.bfloat16


def embed_rows(features, weight):
    raw = jnp.dot(features, weight, preferred_element_type=F32)
    radius = jnp.sqrt(jnp.sum(raw * raw, axis=1, keepdims=True) + EPS)
    unit = raw / radius
    return unit, unit.astype(BF16), radius


def back_norm(unit, radius, gradient):
    along = jnp.sum(unit * gradient, axis=1, keepdims=True)
    return (gradient - unit * along) / radius


def outer_rows(features, direction):
    high = direction.astype(BF16)
    low = (direction - high.astype(F32)).astype(BF16)
    dims = (((0,), (0,)), ((), ()))
    return lax.dot_general(features, high, dims, preferred_element_type=F32) + lax.dot_general(
        features, low, dims, preferred_element_type=F32
    )


def reduce_kernel(
    nx, ny, nz, a_ref, b_ref, oa_ref, ob_ref,
    core_in, first_out, first_in, own, second_out, second_in, last, last_in,
    core_s, core_r, first_s, first_r, second_s, second_r, last_s, last_r,
):
    dp = lax.axis_index("dp")
    z = lax.axis_index("blk")
    core = lax.rem(dp, 2)
    x = lax.rem(dp // 2, nx)
    y = dp // (2 * nx)

    def at(yy, xx, cc, zz):
        return ((yy * nx + xx) * 2 + cc, zz)

    def along_x(k):
        return at(y, lax.rem(x + k, nx), core, z)

    def along_y(k):
        return at(lax.rem(y + k, ny), x, core, z)

    def along_z(k):
        return at(y, x, core, lax.rem(z + k, nz))

    twin = at(y, x, 1 - core, z)
    partners = [twin]
    partners += [along_x(k) for k in range(1, nx)]
    partners += [along_y(k) for k in range(1, ny)]
    partners += [along_z(k) for k in range(1, nz)]
    barrier = pltpu.get_barrier_semaphore()
    for partner in partners:
        pl.semaphore_signal(barrier, inc=1, device_id=partner, device_id_type=MESH)
    pl.semaphore_wait(barrier, len(partners))

    def send(src, dst, s_sem, r_sem, to):
        copy = pltpu.make_async_remote_copy(
            src_ref=src, dst_ref=dst, send_sem=s_sem, recv_sem=r_sem, device_id=to, device_id_type=MESH
        )
        copy.start()
        return copy

    refs = (a_ref, b_ref)
    outs = (oa_ref, ob_ref)
    n1, n2 = (nx, ny), (ny, nx)
    me1, me2 = (x, y), (y, x)
    to1, to2 = (along_x, along_y), (along_y, along_x)

    def place(h, i1, i2):
        return i2 * nx + i1 if h == 0 else i1 * nx + i2

    pending = []
    core_copies = [
        send(refs[h].at[:, 1 - core], core_in.at[h], core_s.at[h], core_r.at[h], twin) for h in range(2)
    ]
    first = [[], []]
    for h in range(2):
        core_copies[h].wait()
        for k in range(1, n1[h]):
            there = lax.rem(me1[h] + k, n1[h])
            for j in range(n2[h]):
                g = place(h, there, j)
                first_out[h, k - 1, j] = (refs[h][g, core] + core_in[h, g]).astype(BF16)
            first[h].append(
                send(first_out.at[h, k - 1], first_in.at[h, k - 1], first_s.at[h, k - 1], first_r.at[h, k - 1], to1[h](k))
            )
        for j in range(n2[h]):
            g = place(h, me1[h], j)
            own[h, j] = refs[h][g, core] + core_in[h, g]
    second = [[], []]
    for h in range(2):
        for copy in first[h]:
            copy.wait()
        for k in range(1, n2[h]):
            there = lax.rem(me2[h] + k, n2[h])
            total = own[h, there]
            for m in range(n1[h] - 1):
                total = total + first_in[h, m, there].astype(F32)
            second_out[h, k - 1] = total.astype(BF16)
            second[h].append(
                send(second_out.at[h, k - 1], second_in.at[h, k - 1], second_s.at[h, k - 1], second_r.at[h, k - 1], to2[h](k))
            )
        total = own[h, me2[h]]
        for m in range(n1[h] - 1):
            total = total + first_in[h, m, me2[h]].astype(F32)
        last[h] = total
    width = oa_ref.shape[1]
    final = [[], []]
    for h in range(2):
        for copy in second[h]:
            copy.wait()
        total = last[h]
        for m in range(n2[h] - 1):
            total = total + second_in[h, m].astype(F32)
        last[h] = total
        for k in range(1, nz):
            columns = pl.ds(pl.multiple_of(lax.rem(z + k, nz) * width, width), width)
            final[h].append(
                send(last.at[h, :, columns], last_in.at[h, k - 1], last_s.at[h, k - 1], last_r.at[h, k - 1], along_z(k))
            )
    for h in range(2):
        for copy in final[h]:
            copy.wait()
        columns = pl.ds(pl.multiple_of(z * width, width), width)
        total = last[h, :, columns]
        for m in range(nz - 1):
            total = total + last_in[h, m]
        outs[h][...] = total


def reduce_heads(head_a, head_b, nx, ny, nz):
    rows, cols = head_a.shape
    groups = nx * ny
    r = rows // (groups * 2)
    shaped = [h.reshape(groups, 2, r, cols) for h in (head_a, head_b)]
    n = max(nx, ny)
    out = jax.ShapeDtypeStruct((r, cols // nz), F32)
    dma = pltpu.SemaphoreType.DMA
    return pl.pallas_call(
        functools.partial(reduce_kernel, nx, ny, nz),
        out_shape=(out, out),
        in_specs=[pl.BlockSpec(memory_space=pltpu.VMEM)] * 2,
        out_specs=(pl.BlockSpec(memory_space=pltpu.VMEM),) * 2,
        scratch_shapes=[
            pltpu.VMEM((2, groups, r, cols), F32),
            pltpu.VMEM((2, n - 1, n, r, cols), BF16),
            pltpu.VMEM((2, n - 1, n, r, cols), BF16),
            pltpu.VMEM((2, n, r, cols), F32),
            pltpu.VMEM((2, n - 1, r, cols), BF16),
            pltpu.VMEM((2, n - 1, r, cols), BF16),
            pltpu.VMEM((2, r, cols), F32),
            pltpu.VMEM((2, nz - 1, r, cols // nz), F32),
            dma((2,)), dma((2,)),
            dma((2, n - 1)), dma((2, n - 1)),
            dma((2, n - 1)), dma((2, n - 1)),
            dma((2, nz - 1)), dma((2, nz - 1)),
        ],
        compiler_params=pltpu.CompilerParams(
            collective_id=0, has_side_effects=True, vmem_limit_bytes=48 * 1024 * 1024
        ),
        name="reduce_heads",
    )(*shaped)


def per_device(nx, ny, prod_feat, prec_feat, matched, row_weight, proj_prod, proj_prec):
    n = lax.axis_size("blk")
    z = lax.axis_index("blk")
    side = [(i, i ^ 1) for i in range(n)]
    across = [(i, n - 1 - i) for i in range(n)]
    own_p, own_c, own_t, own_w = prod_feat[0], prec_feat[0], matched[0], row_weight[0]
    rows = own_p.shape[0]
    far_t = lax.ppermute(own_t, "blk", side)
    far_w = lax.ppermute(own_w, "blk", side)
    far_p = lax.ppermute(own_p, "blk", side)
    far_c = lax.ppermute(own_c, "blk", across)

    feat_p, feat_c = (own_p, far_p), (own_c, far_c)
    targets, weights = (own_t, far_t), (own_w, far_w)
    p = [embed_rows(f, proj_prod) for f in feat_p]
    c = [embed_rows(f, proj_prec) for f in feat_c]
    starts = (z * rows, (n - 1 - z) * rows)

    def scores_of(i, j):
        return LOGIT_SCALE * lax.dot_general(
            p[i][1], c[j][1], (((1,), (1,)), ((), ())), preferred_element_type=F32
        )

    scores = [[scores_of(i, j) for j in range(2)] for i in range(2)]
    matches = [
        [targets[i][:, None] == (starts[j] + lax.iota(jnp.int32, rows))[None, :] for j in range(2)] for i in range(2)
    ]
    part = [sum(jnp.sum(jnp.exp(scores[i][j] - LOGIT_SCALE), axis=1) for j in range(2)) for i in range(2)]
    both = jnp.stack([part[1], part[0]])
    both = lax.ppermute(both, "blk", side)
    totals = [part[0] + both[0], part[1] + both[1]]
    positive = [sum(jnp.sum(jnp.where(matches[i][j], scores[i][j], 0.0), axis=1) for j in range(2)) for i in range(2)]
    loss_local = (
        jnp.sum(own_w * (LOGIT_SCALE + jnp.log(totals[0]))) - jnp.sum(own_w * positive[0]) - jnp.sum(far_w * positive[1])
    )
    loss_sum, weight_total = lax.psum((loss_local, jnp.sum(own_w)), ("dp", "blk"))

    def coeff(i, j):
        probability = jnp.exp(scores[i][j] - LOGIT_SCALE) / totals[i][:, None]
        return (weights[i][:, None] * (probability - matches[i][j].astype(F32))).astype(BF16)

    coeffs = [[coeff(i, j) for j in range(2)] for i in range(2)]
    head_p = head_c = 0.0
    for i in range(2):
        grad = sum(jnp.dot(coeffs[i][j], c[j][1], preferred_element_type=F32) for j in range(2))
        head_p = head_p + outer_rows(feat_p[i], back_norm(p[i][0], p[i][2], LOGIT_SCALE * grad))
    for j in range(2):
        grad = sum(
            lax.dot_general(coeffs[i][j], p[i][1], (((0,), (0,)), ((), ())), preferred_element_type=F32)
            for i in range(2)
        )
        head_c = head_c + outer_rows(feat_c[j], back_norm(c[j][0], c[j][2], LOGIT_SCALE * grad))
    sum_p, sum_c = reduce_heads(head_p, head_c, nx, ny, n)
    return (loss_sum / weight_total, sum_p / weight_total, sum_c / weight_total)


def solution(mesh):
    chips = mesh.shape["dp"] // 2
    ny = math.isqrt(chips)
    nx = chips // ny
    placed = (P("dp", "blk", None), P("dp", "blk", None), P("dp", "blk"), P("dp", "blk"), P(), P())
    return jax.shard_map(
        functools.partial(per_device, nx, ny),
        mesh=mesh,
        in_specs=placed,
        out_specs=(P(), P("dp", "blk"), P("dp", "blk")),
        check_vma=False,
    )
```

```python
import functools
import math

import jax
import jax.numpy as jnp
from jax import lax
from jax.experimental import pallas as pl
from jax.experimental.pallas import tpu as pltpu
from jax.sharding import PartitionSpec as P

EPS = 1e-06
LOGIT_SCALE = 50.0
MESH = pl.DeviceIdType.MESH
F32 = jnp.float32
BF16 = jnp.bfloat16


def embed_rows(features, weight):
    raw = jnp.dot(features, weight, preferred_element_type=F32)
    radius = jnp.sqrt(jnp.sum(raw * raw, axis=1, keepdims=True) + EPS)
    unit = raw / radius
    return unit, unit.astype(BF16), radius


def backward_kernel(
    nx, ny, nz,
    s00, s01, s10, s11, t00, t01, t10, t11, w0, w1, tot0, tot1, rp0, rp1, rc0, rc1,
    up0, up1, uc0, uc1, fp0, fp1, fc0, fc1, stats_ref,
    oa_ref, ob_ref, stats_out,
    coeffs_t, high, low, head, core_in, first_out, first_in, own, second_out, second_in, last, last_in,
    stats_now, stats_in,
    core_s, core_r, first_s, first_r, second_s, second_r, last_s, last_r, stats_s, stats_r,
):
    dp = lax.axis_index("dp")
    z = lax.axis_index("blk")
    core = lax.rem(dp, 2)
    x = lax.rem(dp // 2, nx)
    y = dp // (2 * nx)

    def at(yy, xx, cc, zz):
        return ((yy * nx + xx) * 2 + cc, zz)

    def along_x(k):
        return at(y, lax.rem(x + k, nx), core, z)

    def along_y(k):
        return at(lax.rem(y + k, ny), x, core, z)

    def along_z(k):
        return at(y, x, core, lax.rem(z + k, nz))

    twin = at(y, x, 1 - core, z)
    axes = [
        [twin],
        [along_x(k) for k in range(1, nx)],
        [along_y(k) for k in range(1, ny)],
        [along_z(k) for k in range(1, nz)],
    ]
    partners = sum(axes, [])
    barrier = pltpu.get_barrier_semaphore()
    for partner in partners:
        pl.semaphore_signal(barrier, inc=1, device_id=partner, device_id_type=MESH)
    pl.semaphore_wait(barrier, len(partners))

    def send(src, dst, s_sem, r_sem, to):
        copy = pltpu.make_async_remote_copy(
            src_ref=src, dst_ref=dst, send_sem=s_sem, recv_sem=r_sem, device_id=to, device_id_type=MESH
        )
        copy.start()
        return copy

    def stats_start(axis):
        return [
            send(stats_now.at[axis], stats_in.at[axis, k], stats_s.at[axis, k], stats_r.at[axis, k], to)
            for k, to in enumerate(axes[axis])
        ]

    def stats_end(axis, copies):
        total = stats_now[axis]
        for k, copy in enumerate(copies):
            copy.wait()
            total = total + stats_in[axis, k]
        return total

    rows, feat = fp0.shape
    cols = up0.shape[1]
    groups = nx * ny
    r = feat // (groups * 2)
    width = cols // nz
    half = width // 2

    n1, n2 = (nx, ny), (ny, nx)
    me1, me2 = (x, y), (y, x)
    to1, to2 = (along_x, along_y), (along_y, along_x)

    def head_rows(g, cc):
        return pl.ds(pl.multiple_of((g * 2 + cc) * r, 8), r)

    def core_start(h):
        return [
            send(head.at[h, head_rows(g, 1 - core)], core_in.at[h, g], core_s.at[h, g], core_r.at[h, g], twin)
            for g in range(groups)
        ]

    def place(q, i1, i2):
        return i2 * nx + i1 if q == 0 else i1 * nx + i2

    def piece(h, q, g, zz):
        columns = slice(zz * width + q * half, zz * width + (q + 1) * half)
        return head[h, head_rows(g, core), columns] + core_in[h, g, :, columns]

    def first_start(h, copies):
        for copy in copies:
            copy.wait()
        started = [[], []]
        for q in range(2):
            p = 2 * h + q
            for k in range(1, n1[q]):
                there = lax.rem(me1[q] + k, n1[q])
                for j in range(n2[q]):
                    for zz in range(nz):
                        first_out[p, k - 1, j, :, zz * half:(zz + 1) * half] = piece(h, q, place(q, there, j), zz).astype(BF16)
                started[q].append(
                    send(first_out.at[p, k - 1], first_in.at[p, k - 1], first_s.at[p, k - 1], first_r.at[p, k - 1], to1[q](k))
                )
        for q in range(2):
            for j in range(n2[q]):
                for zz in range(nz):
                    own[2 * h + q, j, :, zz * half:(zz + 1) * half] = piece(h, q, place(q, me1[q], j), zz)
        return started

    def second_start(h, copies):
        started = [[], []]
        for q in range(2):
            p = 2 * h + q
            for copy in copies[q]:
                copy.wait()

            def summed(j):
                total = own[p, j]
                for m in range(n1[q] - 1):
                    total = total + first_in[p, m, j].astype(F32)
                return total

            for k in range(1, n2[q]):
                second_out[p, k - 1] = summed(lax.rem(me2[q] + k, n2[q])).astype(BF16)
                started[q].append(
                    send(second_out.at[p, k - 1], second_in.at[p, k - 1], second_s.at[p, k - 1], second_r.at[p, k - 1], to2[q](k))
                )
            last[p] = summed(me2[q])
        return started

    def last_start(h, copies):
        started = [[], []]
        for q in range(2):
            p = 2 * h + q
            for copy in copies[q]:
                copy.wait()
            total = last[p]
            for m in range(n2[q] - 1):
                total = total + second_in[p, m].astype(F32)
            last[p] = total
            for k in range(1, nz):
                columns = pl.ds(pl.multiple_of(lax.rem(z + k, nz) * half, half), half)
                started[q].append(
                    send(last.at[p, :, columns], last_in.at[p, k - 1], last_s.at[p, k - 1], last_r.at[p, k - 1], along_z(k))
                )
        return started

    def finish(h, copies, out_ref):
        for q in range(2):
            p = 2 * h + q
            for copy in copies[q]:
                copy.wait()
            total = last[p, :, pl.ds(pl.multiple_of(z * half, half), half)]
            for m in range(nz - 1):
                total = total + last_in[p, m]
            out_ref[:, q * half:(q + 1) * half] = total

    scores = ((s00, s01), (s10, s11))
    relative = ((t00, t01), (t10, t11))
    weights, totals = (w0, w1), (tot0, tot1)
    radius_p, radius_c = (rp0, rp1), (rc0, rc1)
    unit_p, unit_c = (up0, up1), (uc0, uc1)
    feat_p, feat_c = (fp0, fp1), (fc0, fc1)
    step = 256

    def directions(grad, unit, radius, where):
        grad = LOGIT_SCALE * grad
        unit = unit.astype(F32)
        direction = (grad - unit * jnp.sum(unit * grad, axis=1, keepdims=True)) / radius
        top = direction.astype(BF16)
        high[where, :] = top
        low[where, :] = (direction - top.astype(F32)).astype(BF16)

    def prod_side(i):
        def body(b, carry):
            start = pl.multiple_of(b * step, step)
            block = pl.ds(start, step)
            grad = None
            for j in range(2):
                probability = jnp.exp(scores[i][j][block, :] - LOGIT_SCALE) / totals[i][block, :]
                match = relative[i][j][block, :] == lax.broadcasted_iota(jnp.int32, (step, rows), 1)
                coeffs = (weights[i][block, :] * (probability - match.astype(F32))).astype(BF16)
                coeffs_t[i, j * rows:(j + 1) * rows, block] = coeffs.T
                term = jnp.dot(coeffs, unit_c[j][...], preferred_element_type=F32)
                grad = term if grad is None else grad + term
            directions(grad, unit_p[i][block, :], radius_p[i][block, :], pl.ds(i * rows + start, step))
            return carry

        lax.fori_loop(0, rows // step, body, 0)

    def prec_side(j):
        def body(b, carry):
            start = pl.multiple_of(b * step, step)
            block = pl.ds(start, step)
            here = pl.ds(j * rows + start, step)
            grad = jnp.dot(coeffs_t[0, here, :], unit_p[0][...], preferred_element_type=F32)
            grad = grad + jnp.dot(coeffs_t[1, here, :], unit_p[1][...], preferred_element_type=F32)
            directions(grad, unit_c[j][block, :], radius_c[j][block, :], here)
            return carry

        lax.fori_loop(0, rows // step, body, 0)

    def outer(h, features):
        def body(b, carry):
            block = pl.ds(pl.multiple_of(b * step, step), step)
            total = None
            for i in range(2):
                turned = features[i][:, block].T
                for term in (high, low):
                    product = jnp.dot(turned, term[i * rows:(i + 1) * rows, :], preferred_element_type=F32)
                    total = product if total is None else total + product
            head[h, block, :] = total
            return carry

        lax.fori_loop(0, feat // step, body, 0)

    stats_now[0] = stats_ref[...]
    small = stats_start(0)
    prod_side(0)
    prod_side(1)
    stats_now[1] = stats_end(0, small)
    small = stats_start(1)
    outer(0, feat_p)
    core_p = core_start(0)
    prec_side(0)
    first_p = first_start(0, core_p)
    stats_now[2] = stats_end(1, small)
    small = stats_start(2)
    prec_side(1)
    second_p = second_start(0, first_p)
    stats_now[3] = stats_end(2, small)
    small = stats_start(3)
    outer(1, feat_c)
    core_c = core_start(1)
    last_p = last_start(0, second_p)
    first_c = first_start(1, core_c)
    second_c = second_start(1, first_c)
    last_c = last_start(1, second_c)
    finish(0, last_p, oa_ref)
    stats_out[...] = stats_end(3, small)
    finish(1, last_c, ob_ref)


def backward(nx, ny, nz, *operands):
    feat = operands[-2].shape[1]
    rows, cols = operands[16].shape
    groups = nx * ny
    r = feat // (groups * 2)
    half = cols // nz // 2
    n = max(nx, ny)
    most = max(n, nz) - 1
    out = jax.ShapeDtypeStruct((r, cols // nz), F32)
    dma = pltpu.SemaphoreType.DMA
    vmem = pl.BlockSpec(memory_space=pltpu.VMEM)
    return pl.pallas_call(
        functools.partial(backward_kernel, nx, ny, nz),
        out_shape=(out, out, jax.ShapeDtypeStruct((8, 128), F32)),
        in_specs=[vmem] * len(operands),
        out_specs=(vmem,) * 3,
        scratch_shapes=[
            pltpu.VMEM((2, 2 * rows, rows), BF16),
            pltpu.VMEM((2 * rows, cols), BF16),
            pltpu.VMEM((2 * rows, cols), BF16),
            pltpu.VMEM((2, feat, cols), F32),
            pltpu.VMEM((2, groups, r, cols), F32),
            pltpu.VMEM((4, n - 1, n, r, cols // 2), BF16),
            pltpu.VMEM((4, n - 1, n, r, cols // 2), BF16),
            pltpu.VMEM((4, n, r, cols // 2), F32),
            pltpu.VMEM((4, n - 1, r, cols // 2), BF16),
            pltpu.VMEM((4, n - 1, r, cols // 2), BF16),
            pltpu.VMEM((4, r, cols // 2), F32),
            pltpu.VMEM((4, nz - 1, r, half), F32),
            pltpu.VMEM((4, 8, 128), F32),
            pltpu.VMEM((4, most, 8, 128), F32),
            dma((2, groups)), dma((2, groups)),
            dma((4, n - 1)), dma((4, n - 1)),
            dma((4, n - 1)), dma((4, n - 1)),
            dma((4, nz - 1)), dma((4, nz - 1)),
            dma((4, most)), dma((4, most)),
        ],
        compiler_params=pltpu.CompilerParams(
            collective_id=0, has_side_effects=True, vmem_limit_bytes=60 * 1024 * 1024
        ),
        name="backward",
    )(*operands)


def per_device(nx, ny, prod_feat, prec_feat, matched, row_weight, proj_prod, proj_prec):
    n = lax.axis_size("blk")
    z = lax.axis_index("blk")
    side = [(i, i ^ 1) for i in range(n)]
    across = [(i, n - 1 - i) for i in range(n)]
    own_p, own_c, own_t, own_w = prod_feat[0], prec_feat[0], matched[0], row_weight[0]
    rows = own_p.shape[0]
    far_t = lax.ppermute(own_t, "blk", side)
    far_w = lax.ppermute(own_w, "blk", side)
    far_p = lax.ppermute(own_p, "blk", side)
    far_c = lax.ppermute(own_c, "blk", across)

    feat_p, feat_c = (own_p, far_p), (own_c, far_c)
    targets, weights = (own_t, far_t), (own_w, far_w)
    p = [embed_rows(f, proj_prod) for f in feat_p]
    c = [embed_rows(f, proj_prec) for f in feat_c]
    starts = (z * rows, (n - 1 - z) * rows)

    def scores_of(i, j):
        return LOGIT_SCALE * lax.dot_general(
            p[i][1], c[j][1], (((1,), (1,)), ((), ())), preferred_element_type=F32
        )

    scores = [[scores_of(i, j) for j in range(2)] for i in range(2)]
    matches = [
        [targets[i][:, None] == (starts[j] + lax.iota(jnp.int32, rows))[None, :] for j in range(2)] for i in range(2)
    ]
    part = [sum(jnp.sum(jnp.exp(scores[i][j] - LOGIT_SCALE), axis=1) for j in range(2)) for i in range(2)]
    both = jnp.stack([part[1], part[0]])
    both = lax.ppermute(both, "blk", side)
    totals = [part[0] + both[0], part[1] + both[1]]
    positive = [sum(jnp.sum(jnp.where(matches[i][j], scores[i][j], 0.0), axis=1) for j in range(2)) for i in range(2)]
    loss_local = (
        jnp.sum(own_w * (LOGIT_SCALE + jnp.log(totals[0]))) - jnp.sum(own_w * positive[0]) - jnp.sum(far_w * positive[1])
    )
    stats = jnp.where(lax.iota(jnp.int32, 8)[:, None] == 0, loss_local, jnp.sum(own_w)) * jnp.ones((8, 128), F32)
    relative = [(targets[i] - starts[j])[:, None] for i in range(2) for j in range(2)]
    sum_p, sum_c, stats = backward(
        nx, ny, n,
        *scores[0], *scores[1], *relative, *(w[:, None] for w in weights), *(t[:, None] for t in totals),
        p[0][2], p[1][2], c[0][2], c[1][2], p[0][1], p[1][1], c[0][1], c[1][1], *feat_p, *feat_c, stats,
    )
    weight_total = stats[1, 0]
    return (stats[0, 0] / weight_total, sum_p / weight_total, sum_c / weight_total)


def solution(mesh):
    chips = mesh.shape["dp"] // 2
    ny = math.isqrt(chips)
    nx = chips // ny
    placed = (P("dp", "blk", None), P("dp", "blk", None), P("dp", "blk"), P("dp", "blk"), P(), P())
    return jax.shard_map(
        functools.partial(per_device, nx, ny),
        mesh=mesh,
        in_specs=placed,
        out_specs=(P(), P("dp", "blk"), P("dp", "blk")),
        check_vma=False,
    )
```

```python
import functools
import math

import jax
import jax.numpy as jnp
from jax import lax
from jax.experimental import pallas as pl
from jax.experimental.pallas import tpu as pltpu
from jax.sharding import PartitionSpec as P

EPS = 1e-06
LOGIT_SCALE = 50.0
MESH = pl.DeviceIdType.MESH
F32 = jnp.float32
BF16 = jnp.bfloat16


def train_kernel(
    nx, ny, nz, own_p, own_c, matched, row_weight, proj_p, proj_c,
    oa_ref, ob_ref, stats_out,
    far_p, far_c, unit, radius, scores, part, pack, pack_in, lines, vecs,
    coeffs_t, high, low, head, core_in, first_out, first_in, own, second_out, second_in, last, last_in,
    stats_now, stats_in,
    far_s, far_r, pack_s, pack_r,
    core_s, core_r, first_s, first_r, second_s, second_r, last_s, last_r, stats_s, stats_r,
):
    dp = lax.axis_index("dp")
    z = lax.axis_index("blk")
    core = lax.rem(dp, 2)
    x = lax.rem(dp // 2, nx)
    y = dp // (2 * nx)

    def at(yy, xx, cc, zz):
        return ((yy * nx + xx) * 2 + cc, zz)

    def along_x(k):
        return at(y, lax.rem(x + k, nx), core, z)

    def along_y(k):
        return at(lax.rem(y + k, ny), x, core, z)

    def along_z(k):
        return at(y, x, core, lax.rem(z + k, nz))

    twin = at(y, x, 1 - core, z)
    axes = [
        [twin],
        [along_x(k) for k in range(1, nx)],
        [along_y(k) for k in range(1, ny)],
        [along_z(k) for k in range(1, nz)],
    ]
    partners = sum(axes, [])
    barrier = pltpu.get_barrier_semaphore()
    for partner in partners:
        pl.semaphore_signal(barrier, inc=1, device_id=partner, device_id_type=MESH)
    pl.semaphore_wait(barrier, len(partners))

    def send(src, dst, s_sem, r_sem, to):
        copy = pltpu.make_async_remote_copy(
            src_ref=src, dst_ref=dst, send_sem=s_sem, recv_sem=r_sem, device_id=to, device_id_type=MESH
        )
        copy.start()
        return copy

    def stats_start(axis):
        return [
            send(stats_now.at[axis], stats_in.at[axis, k], stats_s.at[axis, k], stats_r.at[axis, k], to)
            for k, to in enumerate(axes[axis])
        ]

    def stats_end(axis, copies):
        total = stats_now[axis]
        for k, copy in enumerate(copies):
            copy.wait()
            total = total + stats_in[axis, k]
        return total

    rows, feat = far_p.shape
    cols = unit.shape[2]
    groups = nx * ny
    r = feat // (groups * 2)
    width = cols // nz
    half = width // 2

    n1, n2 = (nx, ny), (ny, nx)
    me1, me2 = (x, y), (y, x)
    to1, to2 = (along_x, along_y), (along_y, along_x)

    def head_rows(g, cc):
        return pl.ds(pl.multiple_of((g * 2 + cc) * r, 8), r)

    def core_start(h):
        return [
            send(head.at[h, head_rows(g, 1 - core)], core_in.at[h, g], core_s.at[h, g], core_r.at[h, g], twin)
            for g in range(groups)
        ]

    def place(q, i1, i2):
        return i2 * nx + i1 if q == 0 else i1 * nx + i2

    def piece(h, q, g, zz):
        columns = slice(zz * width + q * half, zz * width + (q + 1) * half)
        return head[h, head_rows(g, core), columns] + core_in[h, g, :, columns]

    def first_start(h, copies):
        for copy in copies:
            copy.wait()
        started = [[], []]
        for q in range(2):
            p = 2 * h + q
            for k in range(1, n1[q]):
                there = lax.rem(me1[q] + k, n1[q])
                for j in range(n2[q]):
                    for zz in range(nz):
                        first_out[p, k - 1, j, :, zz * half:(zz + 1) * half] = piece(h, q, place(q, there, j), zz).astype(BF16)
                started[q].append(
                    send(first_out.at[p, k - 1], first_in.at[p, k - 1], first_s.at[p, k - 1], first_r.at[p, k - 1], to1[q](k))
                )
        for q in range(2):
            for j in range(n2[q]):
                for zz in range(nz):
                    own[2 * h + q, j, :, zz * half:(zz + 1) * half] = piece(h, q, place(q, me1[q], j), zz)
        return started

    def second_start(h, copies):
        started = [[], []]
        for q in range(2):
            p = 2 * h + q
            for copy in copies[q]:
                copy.wait()

            def summed(j):
                total = own[p, j]
                for m in range(n1[q] - 1):
                    total = total + first_in[p, m, j].astype(F32)
                return total

            for k in range(1, n2[q]):
                second_out[p, k - 1] = summed(lax.rem(me2[q] + k, n2[q])).astype(BF16)
                started[q].append(
                    send(second_out.at[p, k - 1], second_in.at[p, k - 1], second_s.at[p, k - 1], second_r.at[p, k - 1], to2[q](k))
                )
            last[p] = summed(me2[q])
        return started

    def last_start(h, copies):
        started = [[], []]
        for q in range(2):
            p = 2 * h + q
            for copy in copies[q]:
                copy.wait()
            total = last[p]
            for m in range(n2[q] - 1):
                total = total + second_in[p, m].astype(F32)
            last[p] = total
            for k in range(1, nz):
                columns = pl.ds(pl.multiple_of(lax.rem(z + k, nz) * half, half), half)
                started[q].append(
                    send(last.at[p, :, columns], last_in.at[p, k - 1], last_s.at[p, k - 1], last_r.at[p, k - 1], along_z(k))
                )
        return started

    def finish(h, copies, out_ref, weight_total):
        for q in range(2):
            p = 2 * h + q
            for copy in copies[q]:
                copy.wait()
            total = last[p, :, pl.ds(pl.multiple_of(z * half, half), half)]
            for m in range(nz - 1):
                total = total + last_in[p, m]
            out_ref[:, q * half:(q + 1) * half] = total / weight_total

    step = 256
    blocks = rows // step
    local_feat = ((own_p.at[0], far_p), (own_c.at[0], far_c))
    proj = (proj_p, proj_c)

    beside = at(y, x, core, z + 1 - 2 * lax.rem(z, 2))
    across = at(y, x, core, nz - 1 - z)
    arrivals = [[], []]
    for b in range(blocks):
        for side, to in ((0, beside), (1, across)):
            block = pl.ds(b * step, step)
            arrivals[side].append(
                send(local_feat[side][0].at[block, :], local_feat[side][1].at[block, :], far_s.at[side, b], far_r.at[side, b], to)
            )

    def embed(side, i, start):
        block = pl.ds(start, step)
        raw = jnp.dot(local_feat[side][i][block, :], proj[side][...], preferred_element_type=F32)
        length = jnp.sqrt(jnp.sum(raw * raw, axis=1, keepdims=True) + EPS)
        here = pl.ds(i * rows + start, step)
        unit[side, here, :] = (raw / length).astype(BF16)
        radius[side, here, :] = length

    def score(i, p_start, j, c_start, c_count):
        block = pl.ds(p_start, step)
        value = LOGIT_SCALE * lax.dot_general(
            unit[0, pl.ds(i * rows + p_start, step), :],
            unit[1, pl.ds(j * rows + c_start, c_count), :],
            (((1,), (1,)), ((), ())),
            preferred_element_type=F32,
        )
        scores[i, j, block, pl.ds(c_start, c_count)] = value
        part[i, block, :] = part[i, block, :] + jnp.sum(jnp.exp(value - LOGIT_SCALE), axis=1, keepdims=True)

    def each_block(body):
        def run(b, carry):
            body(pl.multiple_of(b * step, step))
            return carry

        lax.fori_loop(0, blocks, run, 0)

    part[...] = jnp.zeros_like(part)
    lines[...] = jnp.zeros_like(lines)
    each_block(lambda start: embed(0, 0, start))
    each_block(lambda start: embed(1, 0, start))
    each_block(lambda start: score(0, start, 0, 0, rows))
    for b in range(blocks):
        arrivals[0][b].wait()
        embed(0, 1, b * step)
        score(1, b * step, 0, 0, rows)
        arrivals[1][b].wait()
        embed(1, 1, b * step)
        each_block(functools.partial(lambda c_start, start: score(0, start, 1, c_start, step), b * step))
    each_block(lambda start: score(1, start, 1, 0, rows))

    lane = lax.broadcasted_iota(jnp.int32, (rows, 128), 1)
    turned_part = jnp.where(lane == 0, part[0], jnp.where(lane == 1, part[1], 0.0)).T
    pack[...] = turned_part[0:8, :]
    pack[2:3, :] = row_weight[...]
    pack[3:4, :] = matched[...].astype(F32)
    exchange = send(pack, pack_in, pack_s, pack_r, beside)
    exchange.wait()
    total_own = pack[0:1, :] + pack_in[1:2, :]
    lines[0:1, :] = pack[2:3, :]
    lines[1:2, :] = pack_in[2:3, :]
    lines[2:3, :] = total_own
    lines[3:4, :] = pack[1:2, :] + pack_in[0:1, :]
    starts = ((z * rows).astype(F32), ((nz - 1 - z) * rows).astype(F32))
    for j in range(2):
        lines[4 + j:5 + j, :] = pack[3:4, :] - starts[j]
        lines[6 + j:7 + j, :] = pack_in[3:4, :] - starts[j]
    vecs[...] = lines[...].T
    numbers = lax.broadcasted_iota(jnp.int32, (1, rows), 1).astype(F32)

    def half_of(side, i):
        return unit[side, i * rows:(i + 1) * rows, :]

    def directions(grad, unit, radius, where):
        grad = LOGIT_SCALE * grad
        unit = unit.astype(F32)
        direction = (grad - unit * jnp.sum(unit * grad, axis=1, keepdims=True)) / radius
        top = direction.astype(BF16)
        high[where, :] = top
        low[where, :] = (direction - top.astype(F32)).astype(BF16)

    def prod_side(i):
        def body(b, matched_sum):
            start = pl.multiple_of(b * step, step)
            block = pl.ds(start, step)
            here = pl.ds(i * rows + start, step)
            weight = vecs[block, i:i + 1]
            total = vecs[block, 2 + i:3 + i]
            grad = None
            for j in range(2):
                value = scores[i, j, block, :]
                match = vecs[block, 4 + 2 * i + j:5 + 2 * i + j] == numbers
                matched_sum = matched_sum + weight * jnp.sum(jnp.where(match, value, 0.0), axis=1, keepdims=True)
                probability = jnp.exp(value - LOGIT_SCALE) / total
                coeffs = (weight * (probability - match.astype(F32))).astype(BF16)
                coeffs_t[i, j * rows:(j + 1) * rows, block] = coeffs.T
                term = jnp.dot(coeffs, half_of(1, j), preferred_element_type=F32)
                grad = term if grad is None else grad + term
            directions(grad, unit[0, here, :], radius[0, here, :], here)
            return matched_sum

        return lax.fori_loop(0, blocks, body, jnp.zeros((step, 1), F32))

    def prec_side(j):
        def body(start):
            here = pl.ds(j * rows + start, step)
            grad = jnp.dot(coeffs_t[0, here, :], half_of(0, 0), preferred_element_type=F32)
            grad = grad + jnp.dot(coeffs_t[1, here, :], half_of(0, 1), preferred_element_type=F32)
            directions(grad, unit[1, here, :], radius[1, here, :], here)

        each_block(body)

    def outer(h, features):
        def body(b, carry):
            block = pl.ds(pl.multiple_of(b * step, step), step)
            total = None
            for i in range(2):
                turned = features[i][:, block].T
                for term in (high, low):
                    product = jnp.dot(turned, term[i * rows:(i + 1) * rows, :], preferred_element_type=F32)
                    total = product if total is None else total + product
            head[h, block, :] = total
            return carry

        lax.fori_loop(0, feat // step, body, 0)

    matched_sum = prod_side(0) + prod_side(1)
    loss = jnp.sum(row_weight[...] * (LOGIT_SCALE + jnp.log(total_own)), axis=1, keepdims=True)
    loss = loss - jnp.sum(matched_sum, axis=0, keepdims=True)
    first_line = lax.broadcasted_iota(jnp.int32, (8, 128), 0) == 0
    stats_now[0] = jnp.where(first_line, loss, jnp.sum(row_weight[...], axis=1, keepdims=True))
    small = stats_start(0)
    outer(0, local_feat[0])
    stats_now[1] = stats_end(0, small)
    small = stats_start(1)
    core_p = core_start(0)
    prec_side(0)
    first_p = first_start(0, core_p)
    stats_now[2] = stats_end(1, small)
    small = stats_start(2)
    prec_side(1)
    second_p = second_start(0, first_p)
    stats_now[3] = stats_end(2, small)
    small = stats_start(3)
    outer(1, local_feat[1])
    core_c = core_start(1)
    last_p = last_start(0, second_p)
    first_c = first_start(1, core_c)
    second_c = second_start(1, first_c)
    last_c = last_start(1, second_c)
    sums = stats_end(3, small)
    weight_total = sums[1:2, 0:1]
    stats_out[...] = sums / weight_total
    finish(0, last_p, oa_ref, weight_total)
    finish(1, last_c, ob_ref, weight_total)


def train(nx, ny, nz, *operands):
    rows, feat = operands[0].shape[1:]
    cols = operands[-1].shape[1]
    step = 256
    groups = nx * ny
    r = feat // (groups * 2)
    half = cols // nz // 2
    n = max(nx, ny)
    most = max(n, nz) - 1
    out = jax.ShapeDtypeStruct((r, cols // nz), F32)
    dma = pltpu.SemaphoreType.DMA
    vmem = pl.BlockSpec(memory_space=pltpu.VMEM)
    return pl.pallas_call(
        functools.partial(train_kernel, nx, ny, nz),
        out_shape=(out, out, jax.ShapeDtypeStruct((8, 128), F32)),
        in_specs=[vmem] * len(operands),
        out_specs=(vmem,) * 3,
        scratch_shapes=[
            pltpu.VMEM((rows, feat), BF16),
            pltpu.VMEM((rows, feat), BF16),
            pltpu.VMEM((2, 2 * rows, cols), BF16),
            pltpu.VMEM((2, 2 * rows, 1), F32),
            pltpu.VMEM((2, 2, rows, rows), F32),
            pltpu.VMEM((2, rows, 1), F32),
            pltpu.VMEM((8, rows), F32),
            pltpu.VMEM((8, rows), F32),
            pltpu.VMEM((128, rows), F32),
            pltpu.VMEM((rows, 128), F32),
            pltpu.VMEM((2, 2 * rows, rows), BF16),
            pltpu.VMEM((2 * rows, cols), BF16),
            pltpu.VMEM((2 * rows, cols), BF16),
            pltpu.VMEM((2, feat, cols), F32),
            pltpu.VMEM((2, groups, r, cols), F32),
            pltpu.VMEM((4, n - 1, n, r, cols // 2), BF16),
            pltpu.VMEM((4, n - 1, n, r, cols // 2), BF16),
            pltpu.VMEM((4, n, r, cols // 2), F32),
            pltpu.VMEM((4, n - 1, r, cols // 2), BF16),
            pltpu.VMEM((4, n - 1, r, cols // 2), BF16),
            pltpu.VMEM((4, r, cols // 2), F32),
            pltpu.VMEM((4, nz - 1, r, half), F32),
            pltpu.VMEM((4, 8, 128), F32),
            pltpu.VMEM((4, most, 8, 128), F32),
            dma((2, rows // step)), dma((2, rows // step)),
            dma, dma,
            dma((2, groups)), dma((2, groups)),
            dma((4, n - 1)), dma((4, n - 1)),
            dma((4, n - 1)), dma((4, n - 1)),
            dma((4, nz - 1)), dma((4, nz - 1)),
            dma((4, most)), dma((4, most)),
        ],
        compiler_params=pltpu.CompilerParams(
            collective_id=0, has_side_effects=True, vmem_limit_bytes=60 * 1024 * 1024
        ),
        name="train",
    )(*operands)


def per_device(nx, ny, *operands):
    sum_p, sum_c, stats = train(nx, ny, lax.axis_size("blk"), *operands)
    return (stats[0, 0], sum_p, sum_c)


def solution(mesh):
    chips = mesh.shape["dp"] // 2
    ny = math.isqrt(chips)
    nx = chips // ny
    placed = (P("dp", "blk", None), P("dp", "blk", None), P("dp", "blk"), P("dp", "blk"), P(), P())
    return jax.shard_map(
        functools.partial(per_device, nx, ny),
        mesh=mesh,
        in_specs=placed,
        out_specs=(P(), P("dp", "blk"), P("dp", "blk")),
        check_vma=False,
    )
```

```python
import functools
import math

import jax
import jax.numpy as jnp
from jax import lax
from jax.experimental import pallas as pl
from jax.experimental.pallas import tpu as pltpu
from jax.sharding import PartitionSpec as P

EPS = 1e-06
LOGIT_SCALE = 50.0
MESH = pl.DeviceIdType.MESH
F32 = jnp.float32
BF16 = jnp.bfloat16


def train_kernel(
    nx, ny, nz, own_p, own_c, matched, row_weight, proj_p, proj_c,
    oa_ref, ob_ref, stats_out,
    far_p, far_c, unit, shrink, scores, part, pack, pack_in, lines, vecs,
    coeffs_t, turns, head, core_in, first_out, first_in, own, second_out, second_in, last, last_in,
    stats_now, stats_in,
    far_s, far_r, pack_s, pack_r,
    core_s, core_r, first_s, first_r, second_s, second_r, last_s, last_r, stats_s, stats_r,
):
    dp = lax.axis_index("dp")
    z = lax.axis_index("blk")
    core = lax.rem(dp, 2)
    x = lax.rem(dp // 2, nx)
    y = dp // (2 * nx)

    def at(yy, xx, cc, zz):
        return ((yy * nx + xx) * 2 + cc, zz)

    def along_x(k):
        return at(y, lax.rem(x + k, nx), core, z)

    def along_y(k):
        return at(lax.rem(y + k, ny), x, core, z)

    def along_z(k):
        return at(y, x, core, lax.rem(z + k, nz))

    twin = at(y, x, 1 - core, z)
    axes = [
        [twin],
        [along_x(k) for k in range(1, nx)],
        [along_y(k) for k in range(1, ny)],
        [along_z(k) for k in range(1, nz)],
    ]
    partners = sum(axes, [])
    barrier = pltpu.get_barrier_semaphore()
    for partner in partners:
        pl.semaphore_signal(barrier, inc=1, device_id=partner, device_id_type=MESH)
    pl.semaphore_wait(barrier, len(partners))

    def send(src, dst, s_sem, r_sem, to):
        copy = pltpu.make_async_remote_copy(
            src_ref=src, dst_ref=dst, send_sem=s_sem, recv_sem=r_sem, device_id=to, device_id_type=MESH
        )
        copy.start()
        return copy

    def stats_start(axis):
        return [
            send(stats_now.at[axis], stats_in.at[axis, k], stats_s.at[axis, k], stats_r.at[axis, k], to)
            for k, to in enumerate(axes[axis])
        ]

    def stats_end(axis, copies):
        total = stats_now[axis]
        for k, copy in enumerate(copies):
            copy.wait()
            total = total + stats_in[axis, k]
        return total

    rows, feat = far_p.shape
    cols = unit.shape[2]
    groups = nx * ny
    r = feat // (groups * 2)
    width = cols // nz
    half = width // 2

    n1, n2 = (nx, ny), (ny, nx)
    me1, me2 = (x, y), (y, x)
    to1, to2 = (along_x, along_y), (along_y, along_x)

    def head_rows(g, cc):
        return pl.ds(pl.multiple_of((g * 2 + cc) * r, 8), r)

    def place(q, i1, i2):
        return i2 * nx + i1 if q == 0 else i1 * nx + i2

    def piece(h, q, g, zz):
        columns = slice(zz * width + q * half, zz * width + (q + 1) * half)
        return head[h, head_rows(g, core), columns] + core_in[h, g, :, columns]

    def first_start(h, copies):
        for copy in copies:
            copy.wait()
        started = [[], []]
        for q in range(2):
            p = 2 * h + q
            for k in range(1, n1[q]):
                there = lax.rem(me1[q] + k, n1[q])
                for j in range(n2[q]):
                    for zz in range(nz):
                        first_out[p, k - 1, j, :, zz * half:(zz + 1) * half] = piece(h, q, place(q, there, j), zz).astype(BF16)
                started[q].append(
                    send(first_out.at[p, k - 1], first_in.at[p, k - 1], first_s.at[p, k - 1], first_r.at[p, k - 1], to1[q](k))
                )
        for q in range(2):
            for j in range(n2[q]):
                for zz in range(nz):
                    own[2 * h + q, j, :, zz * half:(zz + 1) * half] = piece(h, q, place(q, me1[q], j), zz)
        return started

    def second_start(h, copies):
        started = [[], []]
        for q in range(2):
            p = 2 * h + q
            for copy in copies[q]:
                copy.wait()

            def summed(j):
                total = own[p, j]
                for m in range(n1[q] - 1):
                    total = total + first_in[p, m, j].astype(F32)
                return total

            for k in range(1, n2[q]):
                second_out[p, k - 1] = summed(lax.rem(me2[q] + k, n2[q])).astype(BF16)
                started[q].append(
                    send(second_out.at[p, k - 1], second_in.at[p, k - 1], second_s.at[p, k - 1], second_r.at[p, k - 1], to2[q](k))
                )
            last[p] = summed(me2[q])
        return started

    def last_start(h, copies):
        started = [[], []]
        for q in range(2):
            p = 2 * h + q
            for copy in copies[q]:
                copy.wait()
            total = last[p]
            for m in range(n2[q] - 1):
                total = total + second_in[p, m].astype(F32)
            last[p] = total
            for k in range(1, nz):
                columns = pl.ds(pl.multiple_of(lax.rem(z + k, nz) * half, half), half)
                started[q].append(
                    send(last.at[p, :, columns], last_in.at[p, k - 1], last_s.at[p, k - 1], last_r.at[p, k - 1], along_z(k))
                )
        return started

    def finish(h, copies, out_ref, weight_total):
        for q in range(2):
            p = 2 * h + q
            for copy in copies[q]:
                copy.wait()
            total = last[p, :, pl.ds(pl.multiple_of(z * half, half), half)]
            for m in range(nz - 1):
                total = total + last_in[p, m]
            out_ref[:, q * half:(q + 1) * half] = total / weight_total

    step = 256
    blocks = rows // step
    local_feat = ((own_p.at[0], far_p), (own_c.at[0], far_c))
    proj = (proj_p, proj_c)

    beside = at(y, x, core, z + 1 - 2 * lax.rem(z, 2))
    across = at(y, x, core, nz - 1 - z)
    arrivals = [[], []]
    for b in range(blocks):
        for side, to in ((0, beside), (1, across)):
            block = pl.ds(b * step, step)
            arrivals[side].append(
                send(local_feat[side][0].at[block, :], local_feat[side][1].at[block, :], far_s.at[side, b], far_r.at[side, b], to)
            )

    def embed(side, i, start):
        block = pl.ds(start, step)
        raw = jnp.dot(local_feat[side][i][block, :], proj[side][...], preferred_element_type=F32)
        length = jnp.sqrt(jnp.sum(raw * raw, axis=1, keepdims=True) + EPS)
        here = pl.ds(i * rows + start, step)
        inverse = 1.0 / length
        unit[side, here, :] = (raw * inverse).astype(BF16)
        shrink[side, here, :] = LOGIT_SCALE * inverse

    def score(i, p_start, j, c_start, c_count):
        block = pl.ds(p_start, step)
        value = LOGIT_SCALE * lax.dot_general(
            unit[0, pl.ds(i * rows + p_start, step), :],
            unit[1, pl.ds(j * rows + c_start, c_count), :],
            (((1,), (1,)), ((), ())),
            preferred_element_type=F32,
        )
        scores[i, j, block, pl.ds(c_start, c_count)] = value
        part[i, block, :] = part[i, block, :] + jnp.sum(jnp.exp(value - LOGIT_SCALE), axis=1, keepdims=True)

    def each_block(body):
        def run(b, carry):
            body(pl.multiple_of(b * step, step))
            return carry

        lax.fori_loop(0, blocks, run, 0)

    part[...] = jnp.zeros_like(part)
    lines[...] = jnp.zeros_like(lines)
    each_block(lambda start: embed(0, 0, start))
    each_block(lambda start: embed(1, 0, start))
    each_block(lambda start: score(0, start, 0, 0, rows))
    for b in range(blocks):
        arrivals[0][b].wait()
        embed(0, 1, b * step)
        score(1, b * step, 0, 0, rows)
        for done in range(b):
            score(1, b * step, 1, done * step, step)
        arrivals[1][b].wait()
        embed(1, 1, b * step)
        each_block(functools.partial(lambda c_start, start: score(0, start, 1, c_start, step), b * step))
        for done in range(b + 1):
            score(1, done * step, 1, b * step, step)

    lane = lax.broadcasted_iota(jnp.int32, (rows, 128), 1)
    turned_part = jnp.where(lane == 0, part[0], jnp.where(lane == 1, part[1], 0.0)).T
    pack[...] = turned_part[0:8, :]
    pack[2:3, :] = row_weight[...]
    pack[3:4, :] = matched[...].astype(F32)
    exchange = send(pack, pack_in, pack_s, pack_r, beside)
    exchange.wait()
    total_own = pack[0:1, :] + pack_in[1:2, :]
    lines[0:1, :] = pack[2:3, :]
    lines[1:2, :] = pack_in[2:3, :]
    lines[2:3, :] = total_own
    lines[3:4, :] = pack[1:2, :] + pack_in[0:1, :]
    starts = ((z * rows).astype(F32), ((nz - 1 - z) * rows).astype(F32))
    for j in range(2):
        lines[4 + j:5 + j, :] = pack[3:4, :] - starts[j]
        lines[6 + j:7 + j, :] = pack_in[3:4, :] - starts[j]
    vecs[...] = lines[...].T
    numbers = lax.broadcasted_iota(jnp.int32, (1, rows), 1).astype(F32)

    def half_of(side, i):
        return unit[side, i * rows:(i + 1) * rows, :]

    def directions(grad, unit16, scale, where):
        wide = unit16.astype(F32)
        across_unit = grad - wide * jnp.sum(wide * grad, axis=1, keepdims=True)
        turns[where, :] = (across_unit * scale).astype(BF16)

    def prod_side(i):
        def body(b, matched_sum):
            start = pl.multiple_of(b * step, step)
            block = pl.ds(start, step)
            here = pl.ds(i * rows + start, step)
            weight = vecs[block, i:i + 1]
            inverse = 1.0 / vecs[block, 2 + i:3 + i]
            grad = None
            for j in range(2):
                value = scores[i, j, block, :]
                match = vecs[block, 4 + 2 * i + j:5 + 2 * i + j] == numbers
                matched_sum = matched_sum + weight * jnp.sum(jnp.where(match, value, 0.0), axis=1, keepdims=True)
                probability = jnp.exp(value - LOGIT_SCALE) * inverse
                coeffs = (weight * (probability - match.astype(F32))).astype(BF16)
                coeffs_t[i, j * rows:(j + 1) * rows, block] = coeffs.T
                term = jnp.dot(coeffs, half_of(1, j), preferred_element_type=F32)
                grad = term if grad is None else grad + term
            directions(grad, unit[0, here, :], shrink[0, here, :], here)
            return matched_sum

        return lax.fori_loop(0, blocks, body, jnp.zeros((step, 1), F32))

    def prec_side(first, count):
        def body(b, carry):
            here = pl.ds(pl.multiple_of(b * step, step), step)
            grad = jnp.dot(coeffs_t[0, here, :], half_of(0, 0), preferred_element_type=F32)
            grad = grad + jnp.dot(coeffs_t[1, here, :], half_of(0, 1), preferred_element_type=F32)
            directions(grad, unit[1, here, :], shrink[1, here, :], here)
            return carry

        lax.fori_loop(first, first + count, body, 0)

    def outer(h, features):
        copies = []
        for b in range(feat // step):
            block = slice(b * step, (b + 1) * step)
            total = None
            for i in range(2):
                product = jnp.dot(
                    features[i][:, block].T, turns[i * rows:(i + 1) * rows, :], preferred_element_type=F32
                )
                total = product if total is None else total + product
            head[h, block, :] = total
            while len(copies) < groups and (len(copies) + 1) * 2 * r <= (b + 1) * step:
                g = len(copies)
                copies.append(
                    send(head.at[h, head_rows(g, 1 - core)], core_in.at[h, g], core_s.at[h, g], core_r.at[h, g], twin)
                )
        return copies

    matched_sum = prod_side(0) + prod_side(1)
    loss = jnp.sum(row_weight[...] * (LOGIT_SCALE + jnp.log(total_own)), axis=1, keepdims=True)
    loss = loss - jnp.sum(matched_sum, axis=0, keepdims=True)
    first_line = lax.broadcasted_iota(jnp.int32, (8, 128), 0) == 0
    stats_now[0] = jnp.where(first_line, loss, jnp.sum(row_weight[...], axis=1, keepdims=True))
    small = stats_start(0)
    core_p = outer(0, local_feat[0])
    stats_now[1] = stats_end(0, small)
    small = stats_start(1)
    third = 2 * blocks // 3
    prec_side(0, third)
    first_p = first_start(0, core_p)
    stats_now[2] = stats_end(1, small)
    small = stats_start(2)
    prec_side(third, third)
    second_p = second_start(0, first_p)
    stats_now[3] = stats_end(2, small)
    small = stats_start(3)
    prec_side(2 * third, 2 * blocks - 2 * third)
    last_p = last_start(0, second_p)
    core_c = outer(1, local_feat[1])
    first_c = first_start(1, core_c)
    second_c = second_start(1, first_c)
    last_c = last_start(1, second_c)
    sums = stats_end(3, small)
    weight_total = sums[1:2, 0:1]
    stats_out[...] = sums / weight_total
    finish(0, last_p, oa_ref, weight_total)
    finish(1, last_c, ob_ref, weight_total)


def train(nx, ny, nz, *operands):
    rows, feat = operands[0].shape[1:]
    cols = operands[-1].shape[1]
    step = 256
    groups = nx * ny
    r = feat // (groups * 2)
    half = cols // nz // 2
    n = max(nx, ny)
    most = max(n, nz) - 1
    out = jax.ShapeDtypeStruct((r, cols // nz), F32)
    dma = pltpu.SemaphoreType.DMA
    vmem = pl.BlockSpec(memory_space=pltpu.VMEM)
    return pl.pallas_call(
        functools.partial(train_kernel, nx, ny, nz),
        out_shape=(out, out, jax.ShapeDtypeStruct((8, 128), F32)),
        in_specs=[vmem] * len(operands),
        out_specs=(vmem,) * 3,
        scratch_shapes=[
            pltpu.VMEM((rows, feat), BF16),
            pltpu.VMEM((rows, feat), BF16),
            pltpu.VMEM((2, 2 * rows, cols), BF16),
            pltpu.VMEM((2, 2 * rows, 1), F32),
            pltpu.VMEM((2, 2, rows, rows), F32),
            pltpu.VMEM((2, rows, 1), F32),
            pltpu.VMEM((8, rows), F32),
            pltpu.VMEM((8, rows), F32),
            pltpu.VMEM((128, rows), F32),
            pltpu.VMEM((rows, 128), F32),
            pltpu.VMEM((2, 2 * rows, rows), BF16),
            pltpu.VMEM((2 * rows, cols), BF16),
            pltpu.VMEM((2, feat, cols), F32),
            pltpu.VMEM((2, groups, r, cols), F32),
            pltpu.VMEM((4, n - 1, n, r, cols // 2), BF16),
            pltpu.VMEM((4, n - 1, n, r, cols // 2), BF16),
            pltpu.VMEM((4, n, r, cols // 2), F32),
            pltpu.VMEM((4, n - 1, r, cols // 2), BF16),
            pltpu.VMEM((4, n - 1, r, cols // 2), BF16),
            pltpu.VMEM((4, r, cols // 2), F32),
            pltpu.VMEM((4, nz - 1, r, half), F32),
            pltpu.VMEM((4, 8, 128), F32),
            pltpu.VMEM((4, most, 8, 128), F32),
            dma((2, rows // step)), dma((2, rows // step)),
            dma, dma,
            dma((2, groups)), dma((2, groups)),
            dma((4, n - 1)), dma((4, n - 1)),
            dma((4, n - 1)), dma((4, n - 1)),
            dma((4, nz - 1)), dma((4, nz - 1)),
            dma((4, most)), dma((4, most)),
        ],
        compiler_params=pltpu.CompilerParams(
            collective_id=0, has_side_effects=True, vmem_limit_bytes=60 * 1024 * 1024
        ),
        name="train",
    )(*operands)


def per_device(nx, ny, *operands):
    sum_p, sum_c, stats = train(nx, ny, lax.axis_size("blk"), *operands)
    return (stats[0, 0], sum_p, sum_c)


def solution(mesh):
    chips = mesh.shape["dp"] // 2
    ny = math.isqrt(chips)
    nx = chips // ny
    placed = (P("dp", "blk", None), P("dp", "blk", None), P("dp", "blk"), P("dp", "blk"), P(), P())
    return jax.shard_map(
        functools.partial(per_device, nx, ny),
        mesh=mesh,
        in_specs=placed,
        out_specs=(P(), P("dp", "blk"), P("dp", "blk")),
        check_vma=False,
    )
```
